32 devices in a mesh: seq: 8 (over z, x), mp: 4 (over y, core).
Axes of the slice: x: 2, y: 2, z: 4, core: 2. Of those that a mesh axis runs over, the one named last changes fastest.
Arguments:
- store_rows: bfloat16 [4096, 4096], P('seq', 'mp'), may hold values from -6 to 6
- norm_gain: float32 [4096], replicated, may hold values from 0.1 to 1.9
- w_query: bfloat16 [4096, 2048], P(None, 'mp'), may hold values from -0.01171875 to 0.01171875
- w_key: bfloat16 [4096, 2048], P(None, 'mp'), may hold values from -0.09375 to 0.09375
- w_value: bfloat16 [4096, 2048], P(None, 'mp'), may hold values from -0.09375 to 0.09375
- w_out: bfloat16 [2048, 4096], P(None, 'mp'), may hold values from -0.125 to 0.125
- rel_bias: float32 [32, 32], P(None, 'mp'), may hold values from -3 to 251
- lengths: int32 [8], replicated, may hold values from 64 to 512, as said below
- slot_map: int32 [8], replicated, may hold values from 0 to 7, each once
- block_passage: int32 [8, 8], replicated, may hold values from 0 to 7, as said below
- block_index: int32 [8, 8], replicated, may hold values from 0 to 7, as said below
Outputs:
- encoded: bfloat16 [4096, 4096], P('seq', 'mp')
The draws below stay inside these ranges and needn't reach their ends.
Inputs may be any that keep to these rules, and one draw needn't show every extreme that they name: For every passage p and place j there is exactly one store shard s and slot k with block_passage[s, k] = p and block_index[s, k] = j; every row names each passage once. `block_index`: see block_passage. `lengths`: one passage has exactly 512 tokens. `slot_map`: a permutation.
All inputs are finite; a program needn't handle non-finite values.
Results may differ from the reference program's by a relative error of at most 0.0054.
Values may be sent and summed in bfloat16 or wider, within the bound.
A program may use at most 128 MiB of HBM per device.

```python
import math
import jax
import jax.numpy as jnp
import numpy as np
from jax import lax

D = 4096
HEADS = 32
HEAD = 64
LEN = 512
BUCKETS = 32
PASS = 8
BLOCK = 64
N_SEQ = 8


def block_tables(key):
    passage_keys = jax.random.split(jax.random.fold_in(key, 11), PASS)
    shard_of_block = jax.vmap(lambda subkey: jax.random.permutation(subkey, N_SEQ))(passage_keys).astype(jnp.int32)
    inverse = jnp.argsort(shard_of_block, axis=1).astype(jnp.int32)
    shard_keys = jax.random.split(jax.random.fold_in(key, 12), N_SEQ)
    slot_order = jax.vmap(lambda subkey: jax.random.permutation(subkey, PASS))(shard_keys).astype(jnp.int32)
    block_of_shard = inverse[slot_order, jnp.arange(N_SEQ, dtype=jnp.int32)[:, None]]
    return (slot_order, block_of_shard.astype(jnp.int32))


def draw_block_passage(key, part):
    slot_order, block_of_shard = block_tables(key)
    return slot_order


def draw_block_index(key, part):
    slot_order, block_of_shard = block_tables(key)
    return block_of_shard


def draw_lengths(key, part):
    key = jax.random.fold_in(key, 3)
    first_key, second_key = jax.random.split(key)
    base_values = jax.random.randint(first_key, (PASS,), LEN // 8, LEN + 1)
    longest = jax.random.randint(second_key, (), 0, PASS)
    return jnp.where(jnp.arange(PASS) == longest, LEN, base_values).astype(jnp.int32)


def draw_rel_bias(key, part):
    key = jax.random.fold_in(key, 5)
    first_key = jax.random.fold_in(key, 0)
    return jnp.clip(jax.random.normal(first_key, (BUCKETS, HEADS), jnp.float32), -3.0, 3.0)


def block_scale(stream_key, dims, pieces, least, high):
    loudness = 1.0
    for axis_at, shards_of in pieces:
        draws = jax.random.uniform(jax.random.fold_in(jax.random.fold_in(stream_key, 6), axis_at), (shards_of,), jnp.float32, least / len(pieces), high / len(pieces))
        loudness = loudness * jnp.repeat(jnp.exp(draws), dims[axis_at] // shards_of).reshape((-1,) + (1,) * (len(dims) - 1 - axis_at))
    return loudness


def centred(key, dims, spread, reach, cuts=(), held_as=jnp.bfloat16):
    result = spread * jax.random.normal(key, dims, jnp.float32)
    if cuts:
        result = result * block_scale(key, dims, cuts, -0.22, 0.18)
    return jnp.clip(result, -reach, reach).astype(held_as)


def setup_inputs(seed: int = 0) -> dict:
    keys = jax.random.split(jax.random.key(seed), 12)
    return {
        "store_rows": centred(keys[0], (PASS * LEN, D), 1.0, 6.0, ((0, 8), (1, 4))),
        "norm_gain": jnp.clip(1.0 + 0.18 * jax.random.normal(keys[1], (D,), jnp.float32), 0.1, 1.9),
        "w_query": centred(keys[2], (D, HEADS * HEAD), (D * HEAD) ** -0.5, 0.01171875, ((1, 4),)),
        "w_key": centred(keys[3], (D, HEADS * HEAD), D ** -0.5, 0.09375, ((1, 4),)),
        "w_value": centred(keys[4], (D, HEADS * HEAD), D ** -0.5, 0.09375, ((1, 4),)),
        "w_out": centred(keys[5], (HEADS * HEAD, D), (HEADS * HEAD) ** -0.5, 0.125, ((1, 4),)),
        "rel_bias": draw_rel_bias(jax.random.fold_in(keys[11], 71), 0),
        "lengths": draw_lengths(jax.random.fold_in(keys[11], 71), 0),
        "slot_map": jax.random.permutation(keys[8], PASS).astype(jnp.int32),
        "block_passage": draw_block_passage(jax.random.fold_in(keys[11], 71), 0),
        "block_index": draw_block_index(jax.random.fold_in(keys[11], 71), 0),
    }


max_distance = 128

def bucket_of(offset):
    half_count = BUCKETS // 2
    exact_count = BUCKETS // 4
    base_bucket = half_count if offset > 0 else 0
    magnitude = abs(offset)
    if magnitude < exact_count:
        return base_bucket + magnitude
    scaled = math.log(magnitude / exact_count) / math.log(max_distance / exact_count) * (half_count - exact_count)
    return base_bucket + min(exact_count + int(scaled), half_count - 1)

def offset_table(length):
    return np.array([bucket_of(offset) for offset in range(1 - length, length)], dtype=np.int32)

def reference(store_rows, norm_gain, w_query, w_key, w_value, w_out, rel_bias, lengths, slot_map, block_passage, block_index):
    blocks = store_rows.reshape(N_SEQ, PASS, BLOCK, D)
    passages = jnp.zeros((PASS, N_SEQ, BLOCK, D), store_rows.dtype).at[block_passage, block_index].set(blocks)
    passage_order = jnp.argsort(slot_map).astype(jnp.int32)
    seq_rows = passages[passage_order].reshape(PASS, LEN, D)
    seq_lengths = lengths[passage_order]
    table = offset_table(LEN)
    bucket_index = table[np.arange(LEN)[None, :] - np.arange(LEN)[:, None] + LEN - 1]
    position_bias = jnp.transpose(rel_bias[bucket_index], (2, 0, 1)).astype(jnp.float32)

    def encode(packed):
        passage_rows, valid_length = packed
        widened = passage_rows.astype(jnp.float32)
        mean_square = lax.optimization_barrier(jnp.mean(widened * widened, axis=-1, keepdims=True))
        normed = (widened * lax.rsqrt(mean_square + 1e-06) * norm_gain).astype(jnp.bfloat16)
        queries = jnp.dot(normed, w_query, preferred_element_type=jnp.float32).astype(jnp.bfloat16).reshape(LEN, HEADS, HEAD)
        keys_all = jnp.dot(normed, w_key, preferred_element_type=jnp.float32).astype(jnp.bfloat16).reshape(LEN, HEADS, HEAD)
        values = jnp.dot(normed, w_value, preferred_element_type=jnp.float32).astype(jnp.bfloat16).reshape(LEN, HEADS, HEAD)
        scores = jnp.einsum('qhd,khd->hqk', queries.astype(jnp.float32), keys_all.astype(jnp.float32)) + position_bias
        key_valid = jnp.arange(LEN) < valid_length
        scores = jnp.where(key_valid[None, None, :], scores, -jnp.inf)
        row_max = lax.optimization_barrier(jnp.max(scores, axis=-1, keepdims=True))
        weights = jnp.exp(scores - row_max)
        attention_probs = (weights / lax.optimization_barrier(jnp.sum(weights, axis=-1, keepdims=True))).astype(jnp.bfloat16)
        context = jnp.einsum('hqk,khd->qhd', attention_probs.astype(jnp.float32), values.astype(jnp.float32))
        context = context.astype(jnp.bfloat16).reshape(LEN, HEADS * HEAD)
        mixed = jnp.dot(context, w_out, preferred_element_type=jnp.float32) + widened
        return mixed.astype(jnp.bfloat16)
    encoded = lax.map(encode, (seq_rows, seq_lengths))
    return encoded.reshape(PASS * LEN, D)
```

```python
import math

import jax
import jax.numpy as jnp
from jax import lax
from jax.experimental import pallas as pl
from jax.experimental.pallas import tpu as pltpu
from jax.sharding import PartitionSpec as P

HEAD = 64
PAIR = 2 * HEAD
BUCKETS = 32
TILE = 128
GROUPS = 8
MAX_DISTANCE = 128
MESH = pl.DeviceIdType.MESH


def magnitude_bucket(magnitude):
    half_count = BUCKETS // 2
    exact_count = BUCKETS // 4
    if magnitude < exact_count:
        return magnitude
    scaled = (
        math.log(magnitude / exact_count)
        / math.log(MAX_DISTANCE / exact_count)
        * (half_count - exact_count)
    )
    return min(exact_count + int(scaled), half_count - 1)


STARTS = [
    next(m for m in range(MAX_DISTANCE + 1) if magnitude_bucket(m) >= bucket)
    for bucket in range(BUCKETS // 2)
]


def partner_of(index, step, count):
    result = index
    bit = 1
    while bit < count:
        if step & bit:
            result = result + bit * (1 - 2 * (lax.div(index, bit) % 2))
        bit *= 2
    return result


def each(count, body, init):
    if count <= 8:
        for at in range(count):
            init = body(at, init)
        return init
    return lax.fori_loop(0, count, body, init)


def kernel(
    seq_count,
    mp_count,
    store,
    gain,
    rel_bias,
    lengths,
    slot_map,
    block_passage,
    block_index,
    w_query,
    w_key,
    w_value,
    w_out,
    out,
    send,
    recv,
    normed,
    w_in,
    w_last,
    split,
    ordered,
    strips,
    contexts,
    total,
    targets,
    places,
    slots,
    first_send,
    first_recv,
    second_send,
    second_recv,
    context_send,
    context_recv,
    weight_sem,
):
    me = lax.axis_index("seq")
    mine = lax.axis_index("mp")
    _, block_rows, width = store.shape
    length = seq_count * block_rows
    heads_width = w_in.shape[2]
    heads_here = heads_width // HEAD
    pairs = heads_width // PAIR
    chips = mp_count // 2
    per_group = seq_count // GROUPS
    half_slots = seq_count // 2
    half_rows = length // 2
    my_chip = mine // 2
    my_core = mine % 2
    core_peer = my_chip * 2 + 1 - my_core

    def chip_peer(step):
        return ((my_chip + step) % chips) * 2 + my_core

    partners = [partner_of(me, step, seq_count) for step in range(seq_count)]

    barrier = pltpu.get_barrier_semaphore()
    for step in range(1, seq_count):
        pl.semaphore_signal(
            barrier, inc=1, device_id={"seq": partners[step]}, device_id_type=MESH
        )
    for step in range(1, mp_count):
        pl.semaphore_signal(
            barrier,
            inc=1,
            device_id={"mp": (mine + step) % mp_count},
            device_id_type=MESH,
        )

    loads = [
        pltpu.make_async_copy(w_query, w_in.at[0], weight_sem.at[0]),
        pltpu.make_async_copy(w_key, w_in.at[1], weight_sem.at[1]),
        pltpu.make_async_copy(w_value, w_in.at[2], weight_sem.at[2]),
        pltpu.make_async_copy(w_out, w_last, weight_sem.at[3]),
    ]
    for load in loads:
        load.start()

    def find_target(at, carry):
        targets[at] = slot_map[block_passage[me, at]]
        return carry

    each(seq_count, find_target, 0)

    for step in range(seq_count):
        partner = partners[step]
        source = each(
            seq_count,
            lambda at, found: jnp.where(targets[at] == partner, at, found),
            jnp.int32(0),
        )
        if step == 0:
            recv[mine, 0] = store[source]
        else:
            send[step] = store[source]

    pl.semaphore_wait(barrier, seq_count - 1 + mp_count - 1)

    def first_copy(step):
        return pltpu.make_async_remote_copy(
            src_ref=send.at[step],
            dst_ref=recv.at[mine, step],
            send_sem=first_send.at[step],
            recv_sem=first_recv.at[step],
            device_id={"seq": partners[step]},
            device_id_type=MESH,
        )

    near = list(range(1, half_slots))
    far = list(range(half_slots, seq_count))
    order = []
    while near or far:
        if near:
            order.append(near.pop(0))
        if far:
            order.append(far.pop(0))
    for step in order:
        first_copy(step).start()

    def second_copy(group, lane, origin, target):
        part = recv.at[origin, pl.ds(group * per_group, per_group)]
        return pltpu.make_async_remote_copy(
            src_ref=part,
            dst_ref=part,
            send_sem=second_send.at[group, lane],
            recv_sem=second_recv.at[group, origin],
            device_id={"mp": target},
            device_id_type=MESH,
        )

    def handle(group):
        for step in range(group * per_group, (group + 1) * per_group):
            if step > 0:
                first_copy(step).wait_recv()
        for step in range(1, chips):
            second_copy(group, step, mine, chip_peer(step)).start()
        second_copy(group, 0, mine, core_peer).start()

    def relay(group):
        for step in range(1, chips):
            origin = chip_peer(step)
            second_copy(group, step, origin, origin).wait_recv()
            second_copy(group, chips - 1 + step, origin, core_peer).start()

    def complete(group):
        for step in range(chips):
            origin = ((my_chip + step) % chips) * 2 + 1 - my_core
            second_copy(group, 0, origin, core_peer).wait_recv()

    handle(0)

    offset = lax.broadcasted_iota(jnp.int32, (1, 4 * TILE), 1) - 2 * TILE
    distance = jnp.abs(offset)

    def make_strip(head, carry):
        before = jnp.full((1, 4 * TILE), rel_bias[0, head], jnp.float32)
        after = jnp.full((1, 4 * TILE), rel_bias[BUCKETS // 2, head], jnp.float32)
        for bucket in range(1, BUCKETS // 2):
            reached = distance >= STARTS[bucket]
            before = jnp.where(reached, rel_bias[bucket, head], before)
            after = jnp.where(reached, rel_bias[BUCKETS // 2 + bucket, head], after)
        line = jnp.where(offset > 0, after, before)
        wide = jnp.broadcast_to(line, (TILE, 4 * TILE))
        rolled = pltpu.roll(wide, 3 * TILE, 1, stride=1, stride_axis=0)
        strips[head] = rolled[:, : 3 * TILE]
        return carry

    lax.fori_loop(0, heads_here, make_strip, 0)

    handle(1)
    relay(0)

    my_passage = each(
        seq_count,
        lambda at, found: jnp.where(slot_map[at] == me, at, found),
        jnp.int32(0),
    )
    valid_length = lengths[my_passage]
    for step in range(seq_count):
        shard = partners[step]
        places[step] = each(
            seq_count,
            lambda at, found: jnp.where(
                block_passage[shard, at] == my_passage, block_index[shard, at], found
            ),
            jnp.int32(0),
        )

    def find_slot(place, carry):
        slots[place] = each(
            seq_count,
            lambda at, found: jnp.where(places[at] == place, at, found),
            jnp.int32(0),
        )
        return carry

    lax.fori_loop(0, seq_count, find_slot, 0)

    handle(2)
    relay(1)
    handle(3)
    relay(2)

    def normalise(half):
        def one(at, carry):
            slot = half * half_slots + at
            square = jnp.zeros((block_rows, 1), jnp.float32)
            for part in range(mp_count):
                x = recv[part, slot].astype(jnp.float32)
                square = square + jnp.sum(x * x, axis=-1, keepdims=True)
            scale = lax.rsqrt(square / (mp_count * width) + 1e-06)
            rows = pl.ds(pl.multiple_of(slot * block_rows, block_rows), block_rows)
            for part in range(mp_count):
                columns = slice(part * width, (part + 1) * width)
                x = recv[part, slot].astype(jnp.float32)
                normed[rows, columns] = (x * scale * gain[:, columns]).astype(jnp.bfloat16)
            return carry

        lax.fori_loop(0, half_slots, one, 0)

    step_width = min(256, heads_width)

    def project(half, which):
        def one(at, carry):
            columns = pl.ds(pl.multiple_of(at * step_width, step_width), step_width)
            product = jnp.dot(
                normed[half * half_rows : (half + 1) * half_rows, :],
                w_in[which, :, columns],
                preferred_element_type=jnp.float32,
            )
            split[which, half * half_slots : (half + 1) * half_slots, :, columns] = (
                product.astype(jnp.bfloat16).reshape(half_slots, block_rows, step_width)
            )
            return carry

        lax.fori_loop(0, heads_width // step_width, one, 0)

    handle(4)
    relay(3)
    for group in range(4):
        complete(group)
    normalise(0)
    handle(5)
    relay(4)
    loads[0].wait()
    project(0, 0)
    handle(6)
    relay(5)
    loads[1].wait()
    project(0, 1)
    handle(7)
    relay(6)
    loads[2].wait()
    project(0, 2)
    relay(7)
    for group in range(4, 8):
        complete(group)
    normalise(1)
    project(1, 0)
    project(1, 1)
    project(1, 2)

    def arrange(place, carry):
        slot = slots[place]
        rows = pl.ds(pl.multiple_of(place * block_rows, block_rows), block_rows)
        for which in range(3):
            block = split[which, slot]
            for pair in range(pairs):
                ordered[which, pair, rows, :] = block[:, pair * PAIR : (pair + 1) * PAIR]
        return carry

    lax.fori_loop(0, seq_count, arrange, 0)

    key_at = lax.broadcasted_iota(jnp.int32, (1, length), 1)
    blocked = jnp.where(key_at < valid_length, 0.0, -jnp.inf).astype(jnp.float32)
    lane = lax.broadcasted_iota(jnp.int32, (1, PAIR), 1)
    lane_masks = [
        jnp.where(lane // HEAD == at, 1.0, 0.0).astype(jnp.bfloat16) for at in range(2)
    ]
    tiles = length // TILE

    def context_copy(pair, lane_at, origin, target):
        part = contexts.at[origin, pair]
        return pltpu.make_async_remote_copy(
            src_ref=part,
            dst_ref=part,
            send_sem=context_send.at[pair, lane_at],
            recv_sem=context_recv.at[pair, origin],
            device_id={"mp": target},
            device_id_type=MESH,
        )

    def context_relay(pair):
        for step in range(1, chips):
            origin = chip_peer(step)
            context_copy(pair, step, origin, origin).wait_recv()
            context_copy(pair, chips - 1 + step, origin, core_peer).start()

    def attend(pair, carry):
        for row_tile in range(tiles):
            rows = slice(row_tile * TILE, (row_tile + 1) * TILE)
            both = []
            for at in range(2):
                head = pair * 2 + at
                scores = lax.dot_general(
                    ordered[0, pair, rows, :] * lane_masks[at],
                    ordered[1, pair],
                    (((1,), (1,)), ((), ())),
                    preferred_element_type=jnp.float32,
                )
                pieces = []
                for key_tile in range(tiles):
                    columns = slice(key_tile * TILE, (key_tile + 1) * TILE)
                    gap = key_tile - row_tile
                    if gap < -1:
                        bias = rel_bias[BUCKETS // 2 - 1, head]
                    elif gap > 1:
                        bias = rel_bias[BUCKETS - 1, head]
                    else:
                        bias = strips[head, :, (gap + 1) * TILE : (gap + 2) * TILE]
                    pieces.append(scores[:, columns] + bias + blocked[:, columns])
                scores = jnp.concatenate(pieces, axis=1)
                weights = jnp.exp(scores - jnp.max(scores, axis=-1, keepdims=True))
                share = 1.0 / jnp.sum(weights, axis=-1, keepdims=True)
                mixed = jnp.dot(
                    weights.astype(jnp.bfloat16),
                    ordered[2, pair],
                    preferred_element_type=jnp.float32,
                )
                both.append(mixed * share)
            contexts[mine, pair, rows, :] = jnp.where(lane < HEAD, both[0], both[1]).astype(
                jnp.bfloat16
            )
        for step in range(1, chips):
            context_copy(pair, step, mine, chip_peer(step)).start()
        context_copy(pair, 0, mine, core_peer).start()

        @pl.when(pair >= 2)
        def _():
            context_relay(pair - 2)

        return carry

    lax.fori_loop(0, pairs, attend, 0)

    out_width = min(256, width)

    def accumulate(origin, first, last):
        rows = pl.ds(pl.multiple_of(origin * heads_width, heads_width), heads_width)

        def one(at, carry):
            columns = pl.ds(pl.multiple_of(at * out_width, out_width), out_width)
            product = jnp.dot(
                jnp.concatenate([contexts[origin, pair] for pair in range(pairs)], axis=1),
                w_last[rows, columns],
                preferred_element_type=jnp.float32,
            )
            if not first:
                product = product + total[:, columns]
            if last:
                out[:, columns] = product.astype(jnp.bfloat16)
            else:
                total[:, columns] = product
            return carry

        lax.fori_loop(0, width // out_width, one, 0)

    loads[3].wait()
    for pair in range(max(0, pairs - 2), pairs - 1):
        context_relay(pair)
    accumulate(mine, True, False)

    def add_residual(place, carry):
        rows = pl.ds(pl.multiple_of(place * block_rows, block_rows), block_rows)
        total[rows, :] = total[rows, :] + recv[mine, slots[place]].astype(jnp.float32)
        return carry

    lax.fori_loop(0, seq_count, add_residual, 0)
    context_relay(pairs - 1)
    for pair in range(pairs):
        context_copy(pair, 0, core_peer, core_peer).wait_recv()
    accumulate(core_peer, False, chips == 1)
    for step in range(1, chips):
        accumulate(chip_peer(step), False, False)
    for step in range(1, chips):
        origin = ((my_chip + step) % chips) * 2 + 1 - my_core
        for pair in range(pairs):
            context_copy(pair, 0, origin, core_peer).wait_recv()
        accumulate(origin, False, step == chips - 1)

    for step in range(1, seq_count):
        first_copy(step).wait_send()
    for group in range(GROUPS):
        for lane_at in range(mp_count - 1):
            second_copy(group, lane_at, mine, core_peer).wait_send()
    for pair in range(pairs):
        for lane_at in range(mp_count - 1):
            context_copy(pair, lane_at, mine, core_peer).wait_send()


def on_device(seq_count, mp_count, *arguments):
    (
        store_rows,
        norm_gain,
        w_query,
        w_key,
        w_value,
        w_out,
        rel_bias,
        lengths,
        slot_map,
        block_passage,
        block_index,
    ) = arguments
    length, width = store_rows.shape
    block_rows = length // seq_count
    features, heads_width = w_query.shape
    heads_here = heads_width // HEAD
    pairs = heads_width // PAIR
    dma = pltpu.SemaphoreType.DMA
    vmem = pl.BlockSpec(memory_space=pltpu.VMEM)
    smem = pl.BlockSpec(memory_space=pltpu.SMEM)
    anywhere = pl.BlockSpec(memory_space=pl.ANY)

    def body(*refs):
        kernel(seq_count, mp_count, *refs)

    return pl.pallas_call(
        body,
        out_shape=jax.ShapeDtypeStruct((length, width), jnp.bfloat16),
        in_specs=[vmem, vmem] + [smem] * 5 + [anywhere] * 4,
        out_specs=vmem,
        scratch_shapes=[
            pltpu.VMEM((seq_count, block_rows, width), jnp.bfloat16),
            pltpu.VMEM((mp_count, seq_count, block_rows, width), jnp.bfloat16),
            pltpu.VMEM((length, features), jnp.bfloat16),
            pltpu.VMEM((3, features, heads_width), jnp.bfloat16),
            pltpu.VMEM(w_out.shape, jnp.bfloat16),
            pltpu.VMEM((3, seq_count, block_rows, heads_width), jnp.bfloat16),
            pltpu.VMEM((3, pairs, length, PAIR), jnp.bfloat16),
            pltpu.VMEM((heads_here, TILE, 3 * TILE), jnp.float32),
            pltpu.VMEM((mp_count, pairs, length, PAIR), jnp.bfloat16),
            pltpu.VMEM((length, width), jnp.float32),
            pltpu.SMEM((seq_count,), jnp.int32),
            pltpu.SMEM((seq_count,), jnp.int32),
            pltpu.SMEM((seq_count,), jnp.int32),
            dma((seq_count,)),
            dma((seq_count,)),
            dma((GROUPS, mp_count - 1)),
            dma((GROUPS, mp_count)),
            dma((pairs, mp_count - 1)),
            dma((pairs, mp_count)),
            dma((4,)),
        ],
        compiler_params=pltpu.CompilerParams(
            collective_id=0, has_side_effects=True, vmem_limit_bytes=56 * 1024 * 1024
        ),
        name="encoder",
    )(
        store_rows.reshape(seq_count, block_rows, width),
        norm_gain.reshape(1, features),
        rel_bias,
        lengths,
        slot_map,
        block_passage,
        block_index,
        w_query,
        w_key,
        w_value,
        w_out,
    )


def solution(mesh):
    placed = (
        P("seq", "mp"),
        P(),
        P(None, "mp"),
        P(None, "mp"),
        P(None, "mp"),
        P(None, "mp"),
        P(None, "mp"),
        P(),
        P(),
        P(),
        P(),
    )

    def run(*arguments):
        return on_device(mesh.shape["seq"], mesh.shape["mp"], *arguments)

    return jax.shard_map(
        run, mesh=mesh, in_specs=placed, out_specs=P("seq", "mp"), check_vma=False
    )
```

```python
import math

import jax
import jax.numpy as jnp
from jax import lax
from jax.experimental import pallas as pl
from jax.experimental.pallas import tpu as pltpu
from jax.sharding import PartitionSpec as P

HEAD = 64
PAIR = 2 * HEAD
BUCKETS = 32
TILE = 128
GROUPS = 8
MAX_DISTANCE = 128
MESH = pl.DeviceIdType.MESH


def magnitude_bucket(magnitude):
    half_count = BUCKETS // 2
    exact_count = BUCKETS // 4
    if magnitude < exact_count:
        return magnitude
    scaled = (
        math.log(magnitude / exact_count)
        / math.log(MAX_DISTANCE / exact_count)
        * (half_count - exact_count)
    )
    return min(exact_count + int(scaled), half_count - 1)


STARTS = [
    next(m for m in range(MAX_DISTANCE + 1) if magnitude_bucket(m) >= bucket)
    for bucket in range(BUCKETS // 2)
]


def partner_of(index, step, count):
    result = index
    bit = 1
    while bit < count:
        if step & bit:
            result = result + bit * (1 - 2 * (lax.div(index, bit) % 2))
        bit *= 2
    return result


def each(count, body, init):
    if count <= 8:
        for at in range(count):
            init = body(at, init)
        return init
    return lax.fori_loop(0, count, body, init)


def kernel(
    seq_count,
    mp_count,
    store_rows,
    gain_row,
    rel_bias,
    lengths,
    slot_map,
    block_passage,
    block_index,
    w_query,
    w_key,
    w_value,
    w_out,
    out,
    store,
    gain,
    send,
    recv,
    normed,
    w_in,
    w_last,
    split,
    ordered,
    strips,
    contexts,
    total,
    targets,
    places,
    slots,
    first_send,
    first_recv,
    second_send,
    second_recv,
    context_send,
    context_recv,
    weight_sem,
):
    me = lax.axis_index("seq")
    mine = lax.axis_index("mp")
    _, block_rows, width = store.shape
    length = seq_count * block_rows
    heads_width = w_in.shape[2]
    heads_here = heads_width // HEAD
    pairs = heads_width // PAIR
    chips = mp_count // 2
    per_group = seq_count // GROUPS
    half_slots = seq_count // 2
    half_rows = length // 2
    my_chip = mine // 2
    my_core = mine % 2
    core_peer = my_chip * 2 + 1 - my_core

    def chip_peer(step):
        return ((my_chip + step) % chips) * 2 + my_core

    partners = [partner_of(me, step, seq_count) for step in range(seq_count)]

    store_load = pltpu.make_async_copy(store_rows, store, weight_sem.at[4])
    gain_load = pltpu.make_async_copy(gain_row, gain, weight_sem.at[5])
    store_load.start()
    gain_load.start()
    barrier = pltpu.get_barrier_semaphore()
    for step in range(1, seq_count):
        pl.semaphore_signal(
            barrier, inc=1, device_id={"seq": partners[step]}, device_id_type=MESH
        )
    for step in range(1, mp_count):
        pl.semaphore_signal(
            barrier,
            inc=1,
            device_id={"mp": (mine + step) % mp_count},
            device_id_type=MESH,
        )

    loads = [
        pltpu.make_async_copy(w_query, w_in.at[0], weight_sem.at[0]),
        pltpu.make_async_copy(w_key, w_in.at[1], weight_sem.at[1]),
        pltpu.make_async_copy(w_value, w_in.at[2], weight_sem.at[2]),
        pltpu.make_async_copy(w_out, w_last, weight_sem.at[3]),
    ]
    def find_target(at, carry):
        targets[at] = slot_map[block_passage[me, at]]
        return carry

    each(seq_count, find_target, 0)

    def find_source(step):
        return each(
            seq_count,
            lambda at, found: jnp.where(targets[at] == partners[step], at, found),
            jnp.int32(0),
        )

    own_source = find_source(0)
    store_load.wait()
    recv[mine, 0] = store[own_source]
    pl.semaphore_wait(barrier, seq_count - 1 + mp_count - 1)

    def first_copy(step):
        return pltpu.make_async_remote_copy(
            src_ref=send.at[step],
            dst_ref=recv.at[mine, step],
            send_sem=first_send.at[step],
            recv_sem=first_recv.at[step],
            device_id={"seq": partners[step]},
            device_id_type=MESH,
        )

    def second_copy(group, lane, origin, target):
        part = recv.at[origin, pl.ds(group * per_group, per_group)]
        return pltpu.make_async_remote_copy(
            src_ref=part,
            dst_ref=part,
            send_sem=second_send.at[group, lane],
            recv_sem=second_recv.at[group, origin],
            device_id={"mp": target},
            device_id_type=MESH,
        )

    def handle(group):
        for step in range(group * per_group, (group + 1) * per_group):
            if step > 0:
                first_copy(step).wait_recv()
        for step in range(1, chips):
            second_copy(group, step, mine, chip_peer(step)).start()
        second_copy(group, 0, mine, core_peer).start()

    def relay(group):
        for step in range(1, chips):
            origin = chip_peer(step)
            second_copy(group, step, origin, origin).wait_recv()
            second_copy(group, chips - 1 + step, origin, core_peer).start()

    def complete(group):
        for step in range(chips):
            origin = ((my_chip + step) % chips) * 2 + 1 - my_core
            second_copy(group, 0, origin, core_peer).wait_recv()

    near = list(range(1, half_slots))
    far = list(range(half_slots, seq_count))
    order = []
    while near or far:
        if near:
            order.append(near.pop(0))
        if far:
            order.append(far.pop(0))
    if per_group == 1:
        handle(0)
    for step in order:
        send[step] = store[find_source(step)]
        first_copy(step).start()
    if per_group > 1:
        handle(0)
    for load in loads:
        load.start()

    offset = lax.broadcasted_iota(jnp.int32, (1, 4 * TILE), 1) - 2 * TILE
    distance = jnp.abs(offset)

    def make_strip(head, carry):
        before = jnp.full((1, 4 * TILE), rel_bias[head, 0], jnp.float32)
        after = jnp.full((1, 4 * TILE), rel_bias[head, BUCKETS // 2], jnp.float32)
        for bucket in range(1, BUCKETS // 2):
            reached = distance >= STARTS[bucket]
            before = jnp.where(reached, rel_bias[head, bucket], before)
            after = jnp.where(reached, rel_bias[head, BUCKETS // 2 + bucket], after)
        line = jnp.where(offset > 0, after, before)
        wide = jnp.broadcast_to(line, (TILE, 4 * TILE))
        rolled = pltpu.roll(wide, 3 * TILE, 1, stride=1, stride_axis=0)
        strips[head] = rolled[:, : 3 * TILE]
        return carry

    lax.fori_loop(0, heads_here, make_strip, 0)

    handle(1)
    relay(0)

    my_passage = each(
        seq_count,
        lambda at, found: jnp.where(slot_map[at] == me, at, found),
        jnp.int32(0),
    )
    valid_length = lengths[my_passage]
    for step in range(seq_count):
        shard = partners[step]
        places[step] = each(
            seq_count,
            lambda at, found: jnp.where(
                block_passage[shard, at] == my_passage, block_index[shard, at], found
            ),
            jnp.int32(0),
        )

    def find_slot(place, carry):
        slots[place] = each(
            seq_count,
            lambda at, found: jnp.where(places[at] == place, at, found),
            jnp.int32(0),
        )
        return carry

    lax.fori_loop(0, seq_count, find_slot, 0)

    handle(2)
    relay(1)
    handle(3)
    relay(2)

    def normalise(first, count):
        def one(at, carry):
            slot = first * per_group + at
            square = jnp.zeros((block_rows, 1), jnp.float32)
            for part in range(mp_count):
                x = recv[part, slot].astype(jnp.float32)
                square = square + jnp.sum(x * x, axis=-1, keepdims=True)
            scale = lax.rsqrt(square / (mp_count * width) + 1e-06)
            rows = pl.ds(pl.multiple_of(slot * block_rows, block_rows), block_rows)
            for part in range(mp_count):
                columns = slice(part * width, (part + 1) * width)
                x = recv[part, slot].astype(jnp.float32)
                normed[rows, columns] = (x * scale * gain[:, columns]).astype(jnp.bfloat16)
            return carry

        lax.fori_loop(0, count * per_group, one, 0)

    step_width = min(256, heads_width)

    def project(first, count, which, at):
        columns = slice(at * step_width, (at + 1) * step_width)
        part = slice(first * per_group, (first + count) * per_group)
        product = jnp.dot(
            normed[part.start * block_rows : part.stop * block_rows, :],
            w_in[which, :, columns],
            preferred_element_type=jnp.float32,
        )
        split[which, part, :, columns] = product.astype(jnp.bfloat16).reshape(
            count * per_group, block_rows, step_width
        )

    steps = heads_width // step_width

    def project_all(first, count, which):
        for at in range(steps):
            project(first, count, which, at)

    handle(4)
    relay(3)
    handle(5)
    for group in range(4):
        complete(group)
    gain_load.wait()
    normalise(0, 4)
    loads[0].wait()
    project_all(0, 4, 0)
    relay(4)
    loads[1].wait()
    project_all(0, 4, 1)
    handle(6)
    loads[2].wait()
    project_all(0, 4, 2)
    relay(5)
    complete(4)
    complete(5)
    normalise(4, 2)
    project_all(4, 2, 0)
    handle(7)
    relay(6)
    project_all(4, 2, 1)
    project_all(4, 2, 2)
    relay(7)
    complete(6)
    complete(7)
    normalise(6, 2)

    step_pairs = step_width // PAIR

    def arrange(at):
        def one(place, carry):
            slot = slots[place]
            rows = pl.ds(pl.multiple_of(place * block_rows, block_rows), block_rows)
            for which in range(3):
                block = split[which, slot, :, at * step_width : (at + 1) * step_width]
                for pair in range(step_pairs):
                    ordered[which, at * step_pairs + pair, rows, :] = block[
                        :, pair * PAIR : (pair + 1) * PAIR
                    ]
            return carry

        lax.fori_loop(0, seq_count, one, 0)

    key_at = lax.broadcasted_iota(jnp.int32, (1, length), 1)
    blocked = jnp.where(key_at < valid_length, 0.0, -jnp.inf).astype(jnp.float32)
    lane = lax.broadcasted_iota(jnp.int32, (1, PAIR), 1)
    lane_masks = [
        jnp.where(lane // HEAD == at, 1.0, 0.0).astype(jnp.bfloat16) for at in range(2)
    ]
    tiles = length // TILE

    def context_copy(pair, piece, lane_at, origin, target):
        part = contexts.at[origin, pair, pl.ds(piece * half_rows, half_rows)]
        return pltpu.make_async_remote_copy(
            src_ref=part,
            dst_ref=part,
            send_sem=context_send.at[pair, piece, lane_at],
            recv_sem=context_recv.at[pair, piece, origin],
            device_id={"mp": target},
            device_id_type=MESH,
        )

    def context_relay(pair):
        for piece in range(2):
            for step in range(1, chips):
                origin = chip_peer(step)
                context_copy(pair, piece, step, origin, origin).wait_recv()
                context_copy(pair, piece, chips - 1 + step, origin, core_peer).start()

    def attend(pair, carry):
        for row_tile in range(tiles):
            rows = slice(row_tile * TILE, (row_tile + 1) * TILE)
            both = []
            for at in range(2):
                head = pair * 2 + at
                scores = lax.dot_general(
                    ordered[0, pair, rows, :] * lane_masks[at],
                    ordered[1, pair],
                    (((1,), (1,)), ((), ())),
                    preferred_element_type=jnp.float32,
                )
                pieces = []
                for key_tile in range(tiles):
                    columns = slice(key_tile * TILE, (key_tile + 1) * TILE)
                    gap = key_tile - row_tile
                    if gap < -1:
                        bias = rel_bias[head, BUCKETS // 2 - 1]
                    elif gap > 1:
                        bias = rel_bias[head, BUCKETS - 1]
                    else:
                        bias = strips[head, :, (gap + 1) * TILE : (gap + 2) * TILE]
                    pieces.append(scores[:, columns] + bias + blocked[:, columns])
                scores = jnp.concatenate(pieces, axis=1)
                weights = jnp.exp(scores - jnp.max(scores, axis=-1, keepdims=True))
                share = 1.0 / jnp.sum(weights, axis=-1, keepdims=True)
                mixed = jnp.dot(
                    weights.astype(jnp.bfloat16),
                    ordered[2, pair],
                    preferred_element_type=jnp.float32,
                )
                both.append(mixed * share)
            contexts[mine, pair, rows, :] = jnp.where(lane < HEAD, both[0], both[1]).astype(
                jnp.bfloat16
            )
            if (row_tile + 1) % (tiles // 2) == 0:
                piece = row_tile // (tiles // 2)
                for step in range(1, chips):
                    context_copy(pair, piece, step, mine, chip_peer(step)).start()
                context_copy(pair, piece, 0, mine, core_peer).start()

        @pl.when(pair >= 2)
        def _():
            context_relay(pair - 2)

        return carry

    for at in range(steps):
        for which in range(3):
            project(6, 2, which, at)
        arrange(at)
        lax.fori_loop(at * step_pairs, (at + 1) * step_pairs, attend, 0)

    out_width = min(256, width)

    def accumulate(origin, first, last):
        rows = pl.ds(pl.multiple_of(origin * heads_width, heads_width), heads_width)

        def one(at, carry):
            columns = pl.ds(pl.multiple_of(at * out_width, out_width), out_width)
            product = jnp.dot(
                jnp.concatenate([contexts[origin, pair] for pair in range(pairs)], axis=1),
                w_last[rows, columns],
                preferred_element_type=jnp.float32,
            )
            if not first:
                product = product + total[:, columns]
            if last:
                out[:, columns] = product.astype(jnp.bfloat16)
            else:
                total[:, columns] = product
            return carry

        lax.fori_loop(0, width // out_width, one, 0)

    loads[3].wait()
    for pair in range(max(0, pairs - 2), pairs - 1):
        context_relay(pair)
    accumulate(mine, True, False)

    def add_residual(place, carry):
        rows = pl.ds(pl.multiple_of(place * block_rows, block_rows), block_rows)
        total[rows, :] = total[rows, :] + recv[mine, slots[place]].astype(jnp.float32)
        return carry

    lax.fori_loop(0, seq_count, add_residual, 0)
    context_relay(pairs - 1)
    for pair in range(pairs):
        for piece in range(2):
            context_copy(pair, piece, 0, core_peer, core_peer).wait_recv()
    accumulate(core_peer, False, chips == 1)
    for step in range(1, chips):
        accumulate(chip_peer(step), False, False)
    for step in range(1, chips):
        origin = ((my_chip + step) % chips) * 2 + 1 - my_core
        for pair in range(pairs):
            for piece in range(2):
                context_copy(pair, piece, 0, origin, core_peer).wait_recv()
        accumulate(origin, False, step == chips - 1)

    for step in range(1, seq_count):
        first_copy(step).wait_send()
    for group in range(GROUPS):
        for lane_at in range(mp_count - 1):
            second_copy(group, lane_at, mine, core_peer).wait_send()
    for pair in range(pairs):
        for piece in range(2):
            for lane_at in range(mp_count - 1):
                context_copy(pair, piece, lane_at, mine, core_peer).wait_send()


def on_device(seq_count, mp_count, *arguments):
    (
        store_rows,
        norm_gain,
        w_query,
        w_key,
        w_value,
        w_out,
        rel_bias,
        lengths,
        slot_map,
        block_passage,
        block_index,
    ) = arguments
    length, width = store_rows.shape
    block_rows = length // seq_count
    features, heads_width = w_query.shape
    heads_here = heads_width // HEAD
    pairs = heads_width // PAIR
    dma = pltpu.SemaphoreType.DMA
    vmem = pl.BlockSpec(memory_space=pltpu.VMEM)
    smem = pl.BlockSpec(memory_space=pltpu.SMEM)
    anywhere = pl.BlockSpec(memory_space=pl.ANY)

    def body(*refs):
        kernel(seq_count, mp_count, *refs)

    return pl.pallas_call(
        body,
        out_shape=jax.ShapeDtypeStruct((length, width), jnp.bfloat16),
        in_specs=[anywhere] * 2 + [smem] * 5 + [anywhere] * 4,
        out_specs=vmem,
        scratch_shapes=[
            pltpu.VMEM((seq_count, block_rows, width), jnp.bfloat16),
            pltpu.VMEM((1, features), jnp.float32),
            pltpu.VMEM((seq_count, block_rows, width), jnp.bfloat16),
            pltpu.VMEM((mp_count, seq_count, block_rows, width), jnp.bfloat16),
            pltpu.VMEM((length, features), jnp.bfloat16),
            pltpu.VMEM((3, features, heads_width), jnp.bfloat16),
            pltpu.VMEM(w_out.shape, jnp.bfloat16),
            pltpu.VMEM((3, seq_count, block_rows, heads_width), jnp.bfloat16),
            pltpu.VMEM((3, pairs, length, PAIR), jnp.bfloat16),
            pltpu.VMEM((heads_here, TILE, 3 * TILE), jnp.float32),
            pltpu.VMEM((mp_count, pairs, length, PAIR), jnp.bfloat16),
            pltpu.VMEM((length, width), jnp.float32),
            pltpu.SMEM((seq_count,), jnp.int32),
            pltpu.SMEM((seq_count,), jnp.int32),
            pltpu.SMEM((seq_count,), jnp.int32),
            dma((seq_count,)),
            dma((seq_count,)),
            dma((GROUPS, mp_count - 1)),
            dma((GROUPS, mp_count)),
            dma((pairs, 2, mp_count - 1)),
            dma((pairs, 2, mp_count)),
            dma((6,)),
        ],
        compiler_params=pltpu.CompilerParams(
            collective_id=0, has_side_effects=True, vmem_limit_bytes=56 * 1024 * 1024
        ),
        name="encoder",
    )(
        store_rows.reshape(seq_count, block_rows, width),
        norm_gain.reshape(1, features),
        rel_bias.T,
        lengths,
        slot_map,
        block_passage,
        block_index,
        w_query,
        w_key,
        w_value,
        w_out,
    )


def solution(mesh):
    placed = (
        P("seq", "mp"),
        P(),
        P(None, "mp"),
        P(None, "mp"),
        P(None, "mp"),
        P(None, "mp"),
        P(None, "mp"),
        P(),
        P(),
        P(),
        P(),
    )

    def run(*arguments):
        return on_device(mesh.shape["seq"], mesh.shape["mp"], *arguments)

    return jax.shard_map(
        run, mesh=mesh, in_specs=placed, out_specs=P("seq", "mp"), check_vma=False
    )
```

```python
import math

import jax
import jax.numpy as jnp
from jax import lax
from jax.experimental import pallas as pl
from jax.experimental.pallas import tpu as pltpu
from jax.sharding import PartitionSpec as P

HEAD = 64
PAIR = 2 * HEAD
BUCKETS = 32
TILE = 128
GROUPS = 8
MAX_DISTANCE = 128
MESH = pl.DeviceIdType.MESH


def magnitude_bucket(magnitude):
    half_count = BUCKETS // 2
    exact_count = BUCKETS // 4
    if magnitude < exact_count:
        return magnitude
    scaled = (
        math.log(magnitude / exact_count)
        / math.log(MAX_DISTANCE / exact_count)
        * (half_count - exact_count)
    )
    return min(exact_count + int(scaled), half_count - 1)


STARTS = [
    next(m for m in range(MAX_DISTANCE + 1) if magnitude_bucket(m) >= bucket)
    for bucket in range(BUCKETS // 2)
]


def partner_of(index, step, count):
    result = index
    bit = 1
    while bit < count:
        if step & bit:
            result = result + bit * (1 - 2 * (lax.div(index, bit) % 2))
        bit *= 2
    return result


def each(count, body, init):
    if count <= 8:
        for at in range(count):
            init = body(at, init)
        return init
    return lax.fori_loop(0, count, body, init)


def kernel(
    seq_count,
    mp_count,
    store_rows,
    gain_row,
    rel_bias,
    lengths,
    slot_map,
    block_passage,
    block_index,
    w_query,
    w_key,
    w_value,
    w_out,
    out,
    store,
    gain,
    send,
    recv,
    normed,
    w_in,
    w_last,
    split,
    ordered,
    strips,
    contexts,
    total,
    targets,
    places,
    slots,
    first_send,
    first_recv,
    second_send,
    second_recv,
    context_send,
    context_recv,
    weight_sem,
):
    me = lax.axis_index("seq")
    mine = lax.axis_index("mp")
    _, block_rows, width = store.shape
    length = seq_count * block_rows
    heads_width = w_in.shape[2]
    heads_here = heads_width // HEAD
    pairs = heads_width // PAIR
    chips = mp_count // 2
    per_group = seq_count // GROUPS
    half_slots = seq_count // 2
    half_rows = length // 2
    my_chip = mine // 2
    my_core = mine % 2
    core_peer = my_chip * 2 + 1 - my_core

    def chip_peer(step):
        return ((my_chip + step) % chips) * 2 + my_core

    partners = [partner_of(me, step, seq_count) for step in range(seq_count)]

    store_load = pltpu.make_async_copy(store_rows, store, weight_sem.at[4])
    gain_load = pltpu.make_async_copy(gain_row, gain, weight_sem.at[5])
    store_load.start()
    gain_load.start()
    barrier = pltpu.get_barrier_semaphore()
    for step in range(1, seq_count):
        pl.semaphore_signal(
            barrier, inc=1, device_id={"seq": partners[step]}, device_id_type=MESH
        )
    for step in range(1, mp_count):
        pl.semaphore_signal(
            barrier,
            inc=1,
            device_id={"mp": (mine + step) % mp_count},
            device_id_type=MESH,
        )

    loads = [
        pltpu.make_async_copy(w_query, w_in.at[0], weight_sem.at[0]),
        pltpu.make_async_copy(w_key, w_in.at[1], weight_sem.at[1]),
        pltpu.make_async_copy(w_value, w_in.at[2], weight_sem.at[2]),
        pltpu.make_async_copy(w_out, w_last, weight_sem.at[3]),
    ]
    def find_target(at, carry):
        targets[at] = slot_map[block_passage[me, at]]
        return carry

    each(seq_count, find_target, 0)

    def find_source(step):
        return each(
            seq_count,
            lambda at, found: jnp.where(targets[at] == partners[step], at, found),
            jnp.int32(0),
        )

    own_source = find_source(0)
    store_load.wait()
    recv[mine, 0] = store[own_source]
    pl.semaphore_wait(barrier, seq_count - 1 + mp_count - 1)

    def first_copy(step):
        return pltpu.make_async_remote_copy(
            src_ref=send.at[step],
            dst_ref=recv.at[mine, step],
            send_sem=first_send.at[step],
            recv_sem=first_recv.at[step],
            device_id={"seq": partners[step]},
            device_id_type=MESH,
        )

    def second_copy(group, lane, origin, target):
        part = recv.at[origin, pl.ds(group * per_group, per_group)]
        return pltpu.make_async_remote_copy(
            src_ref=part,
            dst_ref=part,
            send_sem=second_send.at[group, lane],
            recv_sem=second_recv.at[group, origin],
            device_id={"mp": target},
            device_id_type=MESH,
        )

    def handle(group):
        for step in range(group * per_group, (group + 1) * per_group):
            if step > 0:
                first_copy(step).wait_recv()
        for step in range(1, chips):
            second_copy(group, step, mine, chip_peer(step)).start()
        second_copy(group, 0, mine, core_peer).start()

    def relay(group):
        for step in range(1, chips):
            origin = chip_peer(step)
            second_copy(group, step, origin, origin).wait_recv()
            second_copy(group, chips - 1 + step, origin, core_peer).start()

    def complete(group):
        for step in range(chips):
            origin = ((my_chip + step) % chips) * 2 + 1 - my_core
            second_copy(group, 0, origin, core_peer).wait_recv()

    near = list(range(1, half_slots))
    far = list(range(half_slots, seq_count))
    order = []
    while near or far:
        if far:
            order.append(far.pop(0))
        if near:
            order.append(near.pop(0))
    if per_group == 1:
        handle(0)
    for step in order:
        send[step] = store[find_source(step)]
        first_copy(step).start()
    if per_group > 1:
        handle(0)
    for load in loads:
        load.start()

    offset = lax.broadcasted_iota(jnp.int32, (1, 4 * TILE), 1) - 2 * TILE
    distance = jnp.abs(offset)

    def make_strip(head, carry):
        before = jnp.full((1, 4 * TILE), rel_bias[head, 0], jnp.float32)
        after = jnp.full((1, 4 * TILE), rel_bias[head, BUCKETS // 2], jnp.float32)
        for bucket in range(1, BUCKETS // 2):
            reached = distance >= STARTS[bucket]
            before = jnp.where(reached, rel_bias[head, bucket], before)
            after = jnp.where(reached, rel_bias[head, BUCKETS // 2 + bucket], after)
        line = jnp.where(offset > 0, after, before)
        wide = jnp.broadcast_to(line, (TILE, 4 * TILE))
        rolled = pltpu.roll(wide, 3 * TILE, 1, stride=1, stride_axis=0)
        strips[head] = rolled[:, : 3 * TILE]
        return carry

    lax.fori_loop(0, heads_here, make_strip, 0)

    handle(1)
    relay(0)

    my_passage = each(
        seq_count,
        lambda at, found: jnp.where(slot_map[at] == me, at, found),
        jnp.int32(0),
    )
    valid_length = lengths[my_passage]
    for step in range(seq_count):
        shard = partners[step]
        places[step] = each(
            seq_count,
            lambda at, found: jnp.where(
                block_passage[shard, at] == my_passage, block_index[shard, at], found
            ),
            jnp.int32(0),
        )

    def find_slot(place, carry):
        slots[place] = each(
            seq_count,
            lambda at, found: jnp.where(places[at] == place, at, found),
            jnp.int32(0),
        )
        return carry

    lax.fori_loop(0, seq_count, find_slot, 0)

    handle(2)
    relay(1)
    handle(3)
    relay(2)

    def normalise(first, count):
        def one(at, carry):
            slot = first * per_group + at
            square = jnp.zeros((block_rows, 1), jnp.float32)
            for part in range(mp_count):
                x = recv[part, slot].astype(jnp.float32)
                square = square + jnp.sum(x * x, axis=-1, keepdims=True)
            scale = lax.rsqrt(square / (mp_count * width) + 1e-06)
            rows = pl.ds(pl.multiple_of(slot * block_rows, block_rows), block_rows)
            for part in range(mp_count):
                columns = slice(part * width, (part + 1) * width)
                x = recv[part, slot].astype(jnp.float32)
                normed[rows, columns] = (x * scale * gain[:, columns]).astype(jnp.bfloat16)
            return carry

        lax.fori_loop(0, count * per_group, one, 0)

    step_width = min(256, heads_width)

    def project(first, count, which, at):
        columns = slice(at * step_width, (at + 1) * step_width)
        part = slice(first * per_group, (first + count) * per_group)
        product = jnp.dot(
            normed[part.start * block_rows : part.stop * block_rows, :],
            w_in[which, :, columns],
            preferred_element_type=jnp.float32,
        )
        split[which, part, :, columns] = product.astype(jnp.bfloat16).reshape(
            count * per_group, block_rows, step_width
        )

    steps = heads_width // step_width

    def project_all(first, count, which):
        for at in range(steps):
            project(first, count, which, at)

    handle(4)
    relay(3)
    handle(5)
    for group in range(4):
        complete(group)
    gain_load.wait()
    normalise(0, 4)
    loads[0].wait()
    project_all(0, 4, 0)
    relay(4)
    loads[1].wait()
    project_all(0, 4, 1)
    handle(6)
    loads[2].wait()
    project_all(0, 4, 2)
    relay(5)
    complete(4)
    complete(5)
    normalise(4, 2)
    project_all(4, 2, 0)
    handle(7)
    relay(6)
    project_all(4, 2, 1)
    project_all(4, 2, 2)
    relay(7)
    complete(6)
    complete(7)
    normalise(6, 2)

    step_pairs = step_width // PAIR

    def arrange(at):
        def one(place, carry):
            slot = slots[place]
            rows = pl.ds(pl.multiple_of(place * block_rows, block_rows), block_rows)
            for which in range(3):
                block = split[which, slot, :, at * step_width : (at + 1) * step_width]
                for pair in range(step_pairs):
                    ordered[which, at * step_pairs + pair, rows, :] = block[
                        :, pair * PAIR : (pair + 1) * PAIR
                    ]
            return carry

        lax.fori_loop(0, seq_count, one, 0)

    key_at = lax.broadcasted_iota(jnp.int32, (1, length), 1)
    blocked = jnp.where(key_at < valid_length, 0.0, -jnp.inf).astype(jnp.float32)
    lane = lax.broadcasted_iota(jnp.int32, (1, PAIR), 1)
    lane_masks = [
        jnp.where(lane // HEAD == at, 1.0, 0.0).astype(jnp.bfloat16) for at in range(2)
    ]
    tiles = length // TILE

    def context_copy(pair, piece, lane_at, origin, target):
        part = contexts.at[origin, pair, pl.ds(piece * half_rows, half_rows)]
        return pltpu.make_async_remote_copy(
            src_ref=part,
            dst_ref=part,
            send_sem=context_send.at[pair, piece, lane_at],
            recv_sem=context_recv.at[pair, piece, origin],
            device_id={"mp": target},
            device_id_type=MESH,
        )

    def context_relay(pair):
        for piece in range(2):
            for step in range(1, chips):
                origin = chip_peer(step)
                context_copy(pair, piece, step, origin, origin).wait_recv()
                context_copy(pair, piece, chips - 1 + step, origin, core_peer).start()

    def attend(pair, carry):
        for row_tile in range(tiles):
            rows = slice(row_tile * TILE, (row_tile + 1) * TILE)
            both = []
            for at in range(2):
                head = pair * 2 + at
                scores = lax.dot_general(
                    ordered[0, pair, rows, :] * lane_masks[at],
                    ordered[1, pair],
                    (((1,), (1,)), ((), ())),
                    preferred_element_type=jnp.float32,
                )
                pieces = []
                for key_tile in range(tiles):
                    columns = slice(key_tile * TILE, (key_tile + 1) * TILE)
                    gap = key_tile - row_tile
                    if gap < -1:
                        bias = rel_bias[head, BUCKETS // 2 - 1]
                    elif gap > 1:
                        bias = rel_bias[head, BUCKETS - 1]
                    else:
                        bias = strips[head, :, (gap + 1) * TILE : (gap + 2) * TILE]
                    pieces.append(scores[:, columns] + bias + blocked[:, columns])
                scores = jnp.concatenate(pieces, axis=1)
                weights = jnp.exp(scores - jnp.max(scores, axis=-1, keepdims=True))
                share = 1.0 / jnp.sum(weights, axis=-1, keepdims=True)
                mixed = jnp.dot(
                    weights.astype(jnp.bfloat16),
                    ordered[2, pair],
                    preferred_element_type=jnp.float32,
                )
                both.append(mixed * share)
            contexts[mine, pair, rows, :] = jnp.where(lane < HEAD, both[0], both[1]).astype(
                jnp.bfloat16
            )
            if (row_tile + 1) % (tiles // 2) == 0:
                piece = row_tile // (tiles // 2)
                for step in range(1, chips):
                    context_copy(pair, piece, step, mine, chip_peer(step)).start()
                context_copy(pair, piece, 0, mine, core_peer).start()

        @pl.when(pair >= 2)
        def _():
            context_relay(pair - 2)

        return carry

    for at in range(steps):
        for which in range(3):
            project(6, 2, which, at)
        arrange(at)
        lax.fori_loop(at * step_pairs, (at + 1) * step_pairs, attend, 0)

    out_width = min(256, width)

    def accumulate(origin, first, last):
        rows = pl.ds(pl.multiple_of(origin * heads_width, heads_width), heads_width)

        def one(at, carry):
            columns = pl.ds(pl.multiple_of(at * out_width, out_width), out_width)
            product = jnp.dot(
                jnp.concatenate([contexts[origin, pair] for pair in range(pairs)], axis=1),
                w_last[rows, columns],
                preferred_element_type=jnp.float32,
            )
            if not first:
                product = product + total[:, columns]
            if last:
                out[:, columns] = product.astype(jnp.bfloat16)
            else:
                total[:, columns] = product
            return carry

        lax.fori_loop(0, width // out_width, one, 0)

    loads[3].wait()
    for pair in range(max(0, pairs - 2), pairs - 1):
        context_relay(pair)
    accumulate(mine, True, False)

    def add_residual(place, carry):
        rows = pl.ds(pl.multiple_of(place * block_rows, block_rows), block_rows)
        total[rows, :] = total[rows, :] + recv[mine, slots[place]].astype(jnp.float32)
        return carry

    lax.fori_loop(0, seq_count, add_residual, 0)
    context_relay(pairs - 1)
    for pair in range(pairs):
        for piece in range(2):
            context_copy(pair, piece, 0, core_peer, core_peer).wait_recv()
    accumulate(core_peer, False, chips == 1)
    for step in range(1, chips):
        accumulate(chip_peer(step), False, False)
    for step in range(1, chips):
        origin = ((my_chip + step) % chips) * 2 + 1 - my_core
        for pair in range(pairs):
            for piece in range(2):
                context_copy(pair, piece, 0, origin, core_peer).wait_recv()
        accumulate(origin, False, step == chips - 1)

    for step in range(1, seq_count):
        first_copy(step).wait_send()
    for group in range(GROUPS):
        for lane_at in range(mp_count - 1):
            second_copy(group, lane_at, mine, core_peer).wait_send()
    for pair in range(pairs):
        for piece in range(2):
            for lane_at in range(mp_count - 1):
                context_copy(pair, piece, lane_at, mine, core_peer).wait_send()


def on_device(seq_count, mp_count, *arguments):
    (
        store_rows,
        norm_gain,
        w_query,
        w_key,
        w_value,
        w_out,
        rel_bias,
        lengths,
        slot_map,
        block_passage,
        block_index,
    ) = arguments
    length, width = store_rows.shape
    block_rows = length // seq_count
    features, heads_width = w_query.shape
    heads_here = heads_width // HEAD
    pairs = heads_width // PAIR
    dma = pltpu.SemaphoreType.DMA
    vmem = pl.BlockSpec(memory_space=pltpu.VMEM)
    smem = pl.BlockSpec(memory_space=pltpu.SMEM)
    anywhere = pl.BlockSpec(memory_space=pl.ANY)

    def body(*refs):
        kernel(seq_count, mp_count, *refs)

    return pl.pallas_call(
        body,
        out_shape=jax.ShapeDtypeStruct((length, width), jnp.bfloat16),
        in_specs=[anywhere] * 2 + [smem] * 5 + [anywhere] * 4,
        out_specs=vmem,
        scratch_shapes=[
            pltpu.VMEM((seq_count, block_rows, width), jnp.bfloat16),
            pltpu.VMEM((1, features), jnp.float32),
            pltpu.VMEM((seq_count, block_rows, width), jnp.bfloat16),
            pltpu.VMEM((mp_count, seq_count, block_rows, width), jnp.bfloat16),
            pltpu.VMEM((length, features), jnp.bfloat16),
            pltpu.VMEM((3, features, heads_width), jnp.bfloat16),
            pltpu.VMEM(w_out.shape, jnp.bfloat16),
            pltpu.VMEM((3, seq_count, block_rows, heads_width), jnp.bfloat16),
            pltpu.VMEM((3, pairs, length, PAIR), jnp.bfloat16),
            pltpu.VMEM((heads_here, TILE, 3 * TILE), jnp.float32),
            pltpu.VMEM((mp_count, pairs, length, PAIR), jnp.bfloat16),
            pltpu.VMEM((length, width), jnp.float32),
            pltpu.SMEM((seq_count,), jnp.int32),
            pltpu.SMEM((seq_count,), jnp.int32),
            pltpu.SMEM((seq_count,), jnp.int32),
            dma((seq_count,)),
            dma((seq_count,)),
            dma((GROUPS, mp_count - 1)),
            dma((GROUPS, mp_count)),
            dma((pairs, 2, mp_count - 1)),
            dma((pairs, 2, mp_count)),
            dma((6,)),
        ],
        compiler_params=pltpu.CompilerParams(
            collective_id=0, has_side_effects=True, vmem_limit_bytes=56 * 1024 * 1024
        ),
        name="encoder",
    )(
        store_rows.reshape(seq_count, block_rows, width),
        norm_gain.reshape(1, features),
        rel_bias.T,
        lengths,
        slot_map,
        block_passage,
        block_index,
        w_query,
        w_key,
        w_value,
        w_out,
    )


def solution(mesh):
    placed = (
        P("seq", "mp"),
        P(),
        P(None, "mp"),
        P(None, "mp"),
        P(None, "mp"),
        P(None, "mp"),
        P(None, "mp"),
        P(),
        P(),
        P(),
        P(),
    )

    def run(*arguments):
        return on_device(mesh.shape["seq"], mesh.shape["mp"], *arguments)

    return jax.shard_map(
        run, mesh=mesh, in_specs=placed, out_specs=P("seq", "mp"), check_vma=False
    )
```
